512 devices in a mesh: group: 32 (over x, z_hi, y), fsdp: 16 (over z_lo, core).
Axes of the slice: x: 4, y: 4, z: 16 (z_hi: 2, z_lo: 8; z = z_hi * 8 + z_lo), core: 2. Of those that a mesh axis runs over, the one named last changes fastest.
Arguments:
- inputs: bfloat16 [32, 2048, 8192], P('group', 'fsdp'), may hold values from -6 to 6
- teacher: bfloat16 [32, 2048, 512], P('group', 'fsdp'), may hold values from -6 to 6
- weight: bfloat16 [32, 8192, 512], P('group', 'fsdp'), may hold values from -6 to 6
- momentum: bfloat16 [32, 8192, 512], P('group', 'fsdp'), may hold values from -6 to 6
- exponent: int32 [4], replicated, may hold values from 0 to 4
Outputs:
- weight_mixed: bfloat16 [32, 8192, 512], P('group', 'fsdp')
- momentum_mixed: bfloat16 [32, 8192, 512], P('group', 'fsdp')
The draws below stay inside these ranges and needn't reach their ends.
All inputs are finite; a program needn't handle non-finite values.
Results may differ from the reference program's by a relative error of at most 0.0073.
Values may be sent and summed in bfloat16 or wider, within the bound.
A program may use at most 64 MiB of HBM per device.

```python
import jax
import jax.numpy as jnp
from jax import lax

D = 8192
KV = 512
ROUNDS = 4
GROUPS = 32
LEVELS = 5
TOK_GROUP = 2048


def touch_ends(entries, key, low, high):
    index_at = [jax.random.randint(jax.random.fold_in(key, axis), (), 0, length) for axis, length in enumerate(entries.shape)]
    main_axis = entries.shape.index(max(entries.shape))
    neighbour = index_at[:main_axis] + [(index_at[main_axis] + 1) % entries.shape[main_axis]] + index_at[main_axis + 1:]
    return entries.at[tuple(index_at)].set(low).at[tuple(neighbour)].set(high)


def block_scale(stream_key, dims, pieces, smallest, largest):
    def one(axis_at, blocks):
        steps = jax.random.uniform(jax.random.fold_in(jax.random.fold_in(stream_key, 6), axis_at), (blocks,), jnp.float32, smallest / len(pieces), largest / len(pieces))
        return jnp.repeat(jnp.exp(steps), dims[axis_at] // blocks).reshape((-1,) + (1,) * (len(dims) - axis_at - 1))

    factor_of = one(*pieces[0])
    for cut in pieces[1:]:
        factor_of = factor_of * one(*cut)
    return factor_of


def bell_draw(key, dims, width, reach, cuts=(), kind=jnp.bfloat16):
    array = jax.random.normal(key, dims, jnp.float32) * width
    if len(cuts) > 0:
        array = block_scale(key, dims, cuts, -0.22, 0.18) * array
    return jnp.clip(array, min=-reach, max=reach).astype(kind)


def setup_inputs(seed: int = 0) -> dict:
    streams_of = jax.random.split(jax.random.key(seed), 6)
    inputs = bell_draw(streams_of[0], (GROUPS, TOK_GROUP, D), 1.0, 6.0, ((0, 32), (1, 16)))
    teacher = bell_draw(streams_of[1], (GROUPS, TOK_GROUP, KV), 1.0, 6.0, ((0, 32), (1, 16)))
    weight = bell_draw(streams_of[2], (GROUPS, D, KV), 1.0, 6.0, ((0, 32), (1, 16)))
    momentum = bell_draw(streams_of[3], (GROUPS, D, KV), 1.0, 6.0, ((0, 32), (1, 16)))
    exponent = touch_ends(jax.random.randint(streams_of[4], (ROUNDS,), 0, LEVELS), jax.random.fold_in(streams_of[4], 1), 0, LEVELS - 1).astype(jnp.int32)
    return dict(inputs=inputs, teacher=teacher, weight=weight, momentum=momentum, exponent=exponent)


MIXES = (0.5, 0.4, 0.3, 0.2)


def one_group(operands):
    inputs, teacher, weight, momentum = operands
    scale = D ** -0.5
    values = jnp.dot(inputs, weight, preferred_element_type=jnp.float32) * scale
    error = (values - teacher.astype(jnp.float32)).astype(jnp.bfloat16)
    grad = jnp.dot(inputs.T, error, preferred_element_type=jnp.float32) * scale
    moved = (0.9 * momentum.astype(jnp.float32) + grad).astype(jnp.bfloat16)
    stepped = (weight.astype(jnp.float32) - 0.05 * moved.astype(jnp.float32)).astype(jnp.bfloat16)
    return stepped, moved


def reference(inputs, teacher, weight, momentum, exponent):
    stepped, moved = lax.map(one_group, (inputs, teacher, weight, momentum))
    groups_ids = jnp.arange(GROUPS, dtype=jnp.int32)
    for rnd in range(ROUNDS):
        weight_c = MIXES[rnd]
        offset = jnp.left_shift(jnp.int32(1), exponent[rnd].astype(jnp.int32))
        partner = jnp.bitwise_xor(groups_ids, offset)
        stepped = ((1.0 - weight_c) * stepped.astype(jnp.float32) + weight_c * stepped[partner].astype(jnp.float32)).astype(jnp.bfloat16)
        moved = ((1.0 - weight_c) * moved.astype(jnp.float32) + weight_c * moved[partner].astype(jnp.float32)).astype(jnp.bfloat16)
    return stepped, moved
```

```python
import functools

import jax
import jax.numpy as jnp
from jax import lax
from jax.experimental import pallas as pl
from jax.experimental.pallas import tpu as pltpu
from jax.sharding import PartitionSpec as P

D = 8192
KV = 512
ROUNDS = 4
MIXES = (0.5, 0.4, 0.3, 0.2)
MESH = pl.DeviceIdType.MESH
F32 = jnp.float32
BF16 = jnp.bfloat16

CHIPS = 8
DEVS = 16
TOK = 128
ROWS = 512
HALF = KV // 2
QW = 128
ITEM = 256
NT = DEVS * TOK // ITEM
NITEM = NT * HALF // QW
SKEW = 2

ORDERS = (("y", 0), ("y", 1), ("x", 0), ("x", 1))
BITS = {"y": (1, 3), "x": (8, 24)}


def blocks(rows, step, body):
    def one(i, carry):
        body(pl.ds(pl.multiple_of(i * step, step), step))
        return carry

    lax.fori_loop(0, rows // step, one, 0)


class Mix:
    def __init__(self, raw, acc, send, recv, ssem, rsem, coef, step):
        self.raw, self.acc, self.send, self.recv = raw, acc, send, recv
        self.ssem, self.rsem, self.coef, self.step = ssem, rsem, coef, step
        self.size = raw.shape[0] // 4

    def axis_of(self, k, stage):
        first, order = ORDERS[k]
        axis = first if stage < 2 else ("x" if first == "y" else "y")
        return axis, order

    def factors(self, k, stage):
        axis, order = self.axis_of(k, stage)
        base = (0 if axis == "y" else 8) + 4 * order
        return [self.coef[base + i] for i in range(4)]

    def copy(self, k, stage):
        axis, order = self.axis_of(k, stage)
        bit = BITS[axis][order if stage % 2 == 0 else 1 - order]
        rows = pl.ds(k * self.size, self.size)
        src = self.raw.at[rows] if stage == 0 else self.send.at[stage - 1, rows]
        return pltpu.make_async_remote_copy(
            src_ref=src,
            dst_ref=self.recv.at[stage, rows],
            send_sem=self.ssem.at[k, stage],
            recv_sem=self.rsem.at[k, stage],
            device_id={"group": lax.axis_index("group") ^ bit},
            device_id_type=MESH,
        )

    def begin(self, k):
        self.copy(k, 0).start()

    def advance(self, k, stage):
        self.copy(k, stage - 1).wait_recv()
        if stage in (1, 3):
            s_own, s_got, o_own, o_got = self.factors(k, stage)

        def body(rows):
            at = pl.ds(k * self.size + rows.start, self.step)
            got = self.recv[stage - 1, at].astype(F32)
            if stage == 1:
                own = self.raw[at].astype(F32)
            else:
                own = self.acc[at]
            if stage in (1, 3):
                self.send[stage - 1, at] = (s_own * own + s_got * got).astype(BF16)
                self.acc[at] = o_own * own + o_got * got
            else:
                total = own + got
                self.acc[at] = total
                if stage == 2:
                    self.send[1, at] = total.astype(BF16)

        blocks(self.size, self.step, body)
        if stage < 4:
            self.copy(k, stage).start()

    def drain(self):
        for k in range(4):
            for stage in range(4):
                self.copy(k, stage).wait_send()


def step_kernel(
    coef, inputs, teacher, weight, momentum, out_w, out_m,
    xc, wm, tc, wm_acc, wm_send, wm_recv, part, right_in, left_in, right_out, left_out,
    gt, g_raw, g_acc, g_send, g_recv, fin,
    a2a_s, a2a_r, fwd_s, fwd_r, own_s, sib_s, sib_r, wm_ss, wm_rs, g_ss, g_rs,
    rs_s, rs_r, ls_s, ls_r, fin_l, fin_s, fin_r,
):
    group, f = lax.axis_index("group"), lax.axis_index("fsdp")
    z, c = f // 2, f % 2
    scale = D ** (-0.5)

    barrier = pltpu.get_barrier_semaphore()

    def greet(i, carry):
        pl.semaphore_signal(
            barrier, inc=1, device_id={"fsdp": (f + i) % DEVS}, device_id_type=MESH
        )
        return carry

    lax.fori_loop(1, DEVS, greet, 0)
    for bit in BITS["y"] + BITS["x"]:
        pl.semaphore_signal(
            barrier, inc=1, device_id={"group": group ^ bit}, device_id_type=MESH
        )
    pl.semaphore_wait(barrier, DEVS - 1 + 4)

    def to_sibling(src, dst, s, r):
        return pltpu.make_async_remote_copy(
            src_ref=src, dst_ref=dst, send_sem=s, recv_sem=r,
            device_id={"fsdp": f ^ 1}, device_id_type=MESH,
        )

    mine = pl.ds(pl.multiple_of(c * HALF, HALF), HALF)
    other = pl.ds(pl.multiple_of((1 - c) * HALF, HALF), HALF)
    w_rows = pl.ds(pl.multiple_of(c * ROWS, ROWS), ROWS)
    m_rows = pl.ds(pl.multiple_of(2 * ROWS + c * ROWS, ROWS), ROWS)
    t_rows = pl.ds(pl.multiple_of(c * TOK, TOK), TOK)
    x_rows = pl.ds(pl.multiple_of(f * TOK, TOK), TOK)
    x_cols = pl.ds(pl.multiple_of(z * 2 * ROWS, 2 * ROWS), 2 * ROWS)
    shared = (
        (weight, mine, other, wm, w_rows),
        (momentum, mine, other, wm, m_rows),
        (teacher, mine, other, tc, t_rows),
        (inputs, x_cols, x_cols, xc, x_rows),
    )
    local = [
        pltpu.make_async_copy(src.at[0, :, keep], dst.at[rows], own_s.at[i])
        for i, (src, keep, _, dst, rows) in enumerate(shared)
    ]
    across = [
        to_sibling(src.at[0, :, give], dst.at[rows], sib_s.at[i], sib_r.at[i])
        for i, (src, _, give, dst, rows) in enumerate(shared)
    ]
    for i in range(2):
        local[i].start()
        across[i].start()

    def far_device(i, ahead):
        return (z + ahead) % CHIPS * 2 + i % 2

    def block(i, there):
        dev = far_device(i, i // 2 if there else CHIPS - i // 2)
        to = dev if there else f
        of = f if there else dev
        return dev, pltpu.make_async_remote_copy(
            src_ref=inputs.at[0, :, pl.ds(pl.multiple_of(to * ROWS, ROWS), ROWS)],
            dst_ref=xc.at[
                pl.ds(pl.multiple_of(of * TOK, TOK), TOK),
                pl.ds(pl.multiple_of((to % 2) * ROWS, ROWS), ROWS),
            ],
            send_sem=a2a_s.at[i],
            recv_sem=a2a_r.at[of],
            device_id={"fsdp": dev},
            device_id_type=MESH,
        )

    def send_block(i, carry):
        block(i, True)[1].start()
        return carry

    lax.fori_loop(2, DEVS, send_block, 0)
    for i in range(2, 4):
        local[i].start()
        across[i].start()

    def zeros(ref):
        ref[...] = jnp.zeros_like(ref)

    pl.when(z == 0)(lambda: zeros(right_in))
    pl.when(z == CHIPS - 1)(lambda: zeros(left_in))
    zeros(gt)

    for i in range(2):
        local[i].wait()
        across[i].wait()
    mix = Mix(wm, wm_acc, wm_send, wm_recv, wm_ss, wm_rs, coef, 64)
    for k in range(4):
        mix.begin(k)
    for stage in range(1, 5):
        for k in range(4):
            mix.advance(k, stage)
    mix.drain()
    for i in range(2, 4):
        local[i].wait()
        across[i].wait()

    def forward(j, cols):
        at = (pl.ds(pl.multiple_of(j * TOK, TOK), TOK), pl.ds(pl.multiple_of(cols * ROWS, ROWS), ROWS))
        return to_sibling(xc.at[at], xc.at[at], fwd_s.at[j], fwd_r.at[j])

    def pass_on(i, carry):
        dev, arrival = block(i, False)
        arrival.wait_recv()
        forward(dev, c).start()
        return carry

    lax.fori_loop(2, DEVS, pass_on, 0)

    def settle(i, carry):
        dev = far_device(i, CHIPS - i // 2)
        forward(dev, c).wait_send()
        forward(dev, 1 - c).wait_recv()
        block(i, True)[1].wait_send()
        return carry

    lax.fori_loop(2, DEVS, settle, 0)

    def share(t, carry):
        rows = pl.ds(pl.multiple_of(t * ITEM, ITEM), ITEM)
        own = jnp.dot(xc[rows], wm[: 2 * ROWS], preferred_element_type=F32) * scale
        for q in range(HALF // QW):
            part[q * NT + t] = own[:, q * QW : (q + 1) * QW]
        return carry

    lax.fori_loop(0, NT, share, 0)
    per_chip = 2 * TOK // ITEM
    for q in range(HALF // QW):
        for i in range(per_chip):
            n = q * NT + z * per_chip + i
            part[n] = part[n] - tc[i * ITEM : (i + 1) * ITEM, q * QW : (q + 1) * QW].astype(F32)

    def hop(n, out, into, s, r, by):
        return pltpu.make_async_remote_copy(
            src_ref=out.at[n], dst_ref=into.at[n], send_sem=s.at[n], recv_sem=r.at[n],
            device_id={"fsdp": (f + DEVS + 2 * by) % DEVS}, device_id_type=MESH,
        )

    def to_right(n):
        return hop(n, right_out, right_in, rs_s, rs_r, 1)

    def to_left(n):
        return hop(n, left_out, left_in, ls_s, ls_r, -1)

    def travel(n, copy, into, out, first, last):
        @pl.when(jnp.logical_and(n >= 0, n < NITEM))
        def _():
            @pl.when(jnp.logical_not(first))
            def _():
                copy(n).wait_recv()

            @pl.when(jnp.logical_not(last))
            def _():
                out[n] = (part[n] + into[n].astype(F32)).astype(BF16)
                copy(n).start()

    far = jnp.maximum(z, CHIPS - 1 - z)

    def step(s, carry):
        travel(s - SKEW * z, to_right, right_in, right_out, z == 0, z == CHIPS - 1)
        travel(s - SKEW * (CHIPS - 1 - z), to_left, left_in, left_out, z == CHIPS - 1, z == 0)
        n = s - SKEW * far

        @pl.when(jnp.logical_and(n >= 0, n < NITEM))
        def _():
            error = (part[n] + right_in[n].astype(F32) + left_in[n].astype(F32)).astype(BF16)
            q, t = n // NT, n % NT
            rows = pl.ds(pl.multiple_of(t * ITEM, ITEM), ITEM)
            gt[q] += lax.dot_general(
                error, xc[rows], (((0,), (0,)), ((), ())), preferred_element_type=F32
            )

        return carry

    lax.fori_loop(0, NITEM + SKEW * (CHIPS - 1), step, 0)

    def sent(n, carry):
        pl.when(z < CHIPS - 1)(lambda: to_right(n).wait_send())
        pl.when(z > 0)(lambda: to_left(n).wait_send())
        return carry

    lax.fori_loop(0, NITEM, sent, 0)

    for q in range(HALF // QW):
        g_raw[:, q * QW : (q + 1) * QW] = (gt[q] * scale).T.astype(BF16)
    mix = Mix(g_raw, g_acc, g_send, g_recv, g_ss, g_rs, coef, 64)
    for k in range(4):
        mix.begin(k)
    for stage in range(1, 5):
        for k in range(4):
            mix.advance(k, stage)

    def finish(rows):
        moved = 0.9 * wm_acc[pl.ds(2 * ROWS + rows.start, 64)] + g_acc[rows]
        fin[1, rows] = moved.astype(BF16)
        fin[0, rows] = (wm_acc[rows] - 0.05 * moved).astype(BF16)

    blocks(2 * ROWS, 64, finish)
    o_rows = pl.ds(pl.multiple_of((1 - c) * ROWS, ROWS), ROWS)
    ends = []
    for i, out in enumerate((out_w, out_m)):
        ends.append(to_sibling(fin.at[i, o_rows], out.at[0, :, mine], fin_s.at[i], fin_r.at[i]))
        ends.append(pltpu.make_async_copy(fin.at[i, w_rows], out.at[0, :, mine], fin_l.at[i]))
    for copy in ends:
        copy.start()
    mix.drain()
    for copy in ends:
        copy.wait()


def step_call(coef, inputs, teacher, weight, momentum):
    dma = lambda *n: pltpu.SemaphoreType.DMA(n)
    anywhere = pl.BlockSpec(memory_space=pl.ANY)
    shape = jax.ShapeDtypeStruct((1, ROWS, KV), BF16)
    rows = 2 * ROWS
    return pl.pallas_call(
        step_kernel,
        name="step",
        out_shape=(shape, shape),
        in_specs=[pl.BlockSpec(memory_space=pltpu.SMEM)] + [anywhere] * 4,
        out_specs=(anywhere, anywhere),
        scratch_shapes=[
            pltpu.VMEM((DEVS * TOK, rows), BF16),
            pltpu.VMEM((2 * rows, HALF), BF16),
            pltpu.VMEM((2 * TOK, HALF), BF16),
            pltpu.VMEM((2 * rows, HALF), F32),
            pltpu.VMEM((3, 2 * rows, HALF), BF16),
            pltpu.VMEM((4, 2 * rows, HALF), BF16),
            pltpu.VMEM((NITEM, ITEM, QW), F32),
            pltpu.VMEM((NITEM, ITEM, QW), BF16),
            pltpu.VMEM((NITEM, ITEM, QW), BF16),
            pltpu.VMEM((NITEM, ITEM, QW), BF16),
            pltpu.VMEM((NITEM, ITEM, QW), BF16),
            pltpu.VMEM((HALF // QW, QW, rows), F32),
            pltpu.VMEM((rows, HALF), BF16),
            pltpu.VMEM((rows, HALF), F32),
            pltpu.VMEM((3, rows, HALF), BF16),
            pltpu.VMEM((4, rows, HALF), BF16),
            pltpu.VMEM((2, rows, HALF), BF16),
            dma(DEVS), dma(DEVS), dma(DEVS), dma(DEVS),
            dma(4), dma(4), dma(4),
            dma(4, 4), dma(4, 4), dma(4, 4), dma(4, 4),
            dma(NITEM), dma(NITEM), dma(NITEM), dma(NITEM),
            dma(2), dma(2), dma(2),
        ],
        compiler_params=pltpu.CompilerParams(
            collective_id=0, has_side_effects=True, vmem_limit_bytes=56 * 2**20
        ),
    )(coef, inputs, teacher, weight, momentum)


def far_kernel(parts, factor, a_ref, b_ref, oa_ref, ob_ref, got, ss, rs):
    partner = lax.axis_index("group") ^ 4
    barrier = pltpu.get_barrier_semaphore()
    pl.semaphore_signal(barrier, inc=1, device_id={"group": partner}, device_id_type=MESH)
    pl.semaphore_wait(barrier, 1)
    size = ROWS // parts
    copies = []
    for i, ref in enumerate((a_ref, b_ref)):
        for j in range(parts):
            rows = pl.ds(j * size, size)
            copies.append(
                pltpu.make_async_remote_copy(
                    src_ref=ref.at[0, rows], dst_ref=got.at[i, rows],
                    send_sem=ss.at[i * parts + j], recv_sem=rs.at[i * parts + j],
                    device_id={"group": partner}, device_id_type=MESH,
                )
            )
            copies[-1].start()
    own, far = factor[0], factor[1]
    for i, (ref, out) in enumerate(((a_ref, oa_ref), (b_ref, ob_ref))):
        for j in range(parts):
            copies[i * parts + j].wait()

            def body(rows):
                at = pl.ds(j * size + rows.start, 64)
                out[0, at] = (own * ref[0, at].astype(F32) + far * got[i, at].astype(F32)).astype(BF16)

            blocks(size, 64, body)


def far_call(factor, a, b):
    parts = 2
    shape = jax.ShapeDtypeStruct((1, ROWS, KV), BF16)
    vmem = pl.BlockSpec(memory_space=pltpu.VMEM)
    return pl.pallas_call(
        functools.partial(far_kernel, parts),
        name="far",
        out_shape=(shape, shape),
        in_specs=[pl.BlockSpec(memory_space=pltpu.SMEM), vmem, vmem],
        out_specs=(vmem, vmem),
        scratch_shapes=[
            pltpu.VMEM((2, ROWS, KV), BF16),
            pltpu.SemaphoreType.DMA((2 * parts,)),
            pltpu.SemaphoreType.DMA((2 * parts,)),
        ],
        compiler_params=pltpu.CompilerParams(
            collective_id=1, has_side_effects=True, vmem_limit_bytes=24 * 2**20
        ),
    )(factor, a, b)


def per_device(inputs, teacher, weight, momentum, exponent):
    levels = jnp.arange(5, dtype=jnp.int32)
    keep = jnp.asarray([1.0 - 2.0 * m for m in MIXES], F32)
    left = jnp.prod(jnp.where(exponent[None, :] == levels[:, None], keep[None, :], 1.0), axis=1)
    own, far = (1.0 + left) * 0.5, (1.0 - left) * 0.5
    coef = []
    for low, high in ((0, 1), (3, 4)):
        a0, b0, a1, b1 = own[low], far[low], own[high], far[high]
        coef += [b0 * b1, a0 * b1, a0 * a1, b0 * a1]
        coef += [b0 * a1, a0 * b1, a0 * a1, b0 * b1]
    pair = step_call(jnp.stack(coef), inputs, teacher, weight, momentum)
    factor = jnp.stack([own[2], far[2]])
    return lax.cond(
        jnp.any(exponent == 2),
        lambda a, b: tuple(far_call(factor, a, b)),
        lambda a, b: (a, b),
        *pair,
    )


def solution(mesh):
    return jax.shard_map(
        per_device,
        mesh=mesh,
        in_specs=(
            P("group", "fsdp", None),
            P("group", "fsdp", None),
            P("group", "fsdp", None),
            P("group", "fsdp", None),
            P(),
        ),
        out_specs=(P("group", "fsdp", None), P("group", "fsdp", None)),
        check_vma=False,
    )
```

```python
import functools

import jax
import jax.numpy as jnp
from jax import lax
from jax.experimental import pallas as pl
from jax.experimental.pallas import tpu as pltpu
from jax.sharding import PartitionSpec as P

D = 8192
KV = 512
ROUNDS = 4
MIXES = (0.5, 0.4, 0.3, 0.2)
MESH = pl.DeviceIdType.MESH
F32 = jnp.float32
BF16 = jnp.bfloat16

CHIPS = 8
DEVS = 16
TOK = 128
ROWS = 512
HALF = KV // 2
QW = 128
ITEM = 256
NT = DEVS * TOK // ITEM
NQ = HALF // QW
NOWN = NT * NQ
NITEM = 2 * NOWN
SKEW = 4
MARGIN = 2
LATE = 1
GAP = 4

ORDERS = (("y", 0), ("y", 1), ("x", 0), ("x", 1))
BITS = {"y": (1, 3), "x": (8, 24)}
LEVELS = {"y": (0, 1), "x": (3, 4)}
FAR_LEVEL = 2


def blocks(rows, step, body):
    def one(i, carry):
        body(pl.ds(pl.multiple_of(i * step, step), step))
        return carry

    lax.fori_loop(0, rows // step, one, 0)


class Mix:
    def __init__(self, raw, acc, send, recv, ssem, rsem, coef, step):
        self.raw, self.acc, self.send, self.recv = raw, acc, send, recv
        self.ssem, self.rsem, self.coef, self.step = ssem, rsem, coef, step
        self.size = raw.shape[0] // 4

    def axis_of(self, k, stage):
        first, order = ORDERS[k]
        axis = first if stage < 2 else ("x" if first == "y" else "y")
        return axis, order

    def factors(self, k, stage):
        axis, order = self.axis_of(k, stage)
        (a0, b0), (a1, b1) = (self.coef[level] for level in LEVELS[axis])
        if order == 0:
            return b0 * b1, a0 * b1, a0 * a1, b0 * a1
        return b0 * a1, a0 * b1, a0 * a1, b0 * b1

    def copy(self, k, stage):
        axis, order = self.axis_of(k, stage)
        bit = BITS[axis][order if stage % 2 == 0 else 1 - order]
        rows = pl.ds(k * self.size, self.size)
        src = self.raw.at[rows] if stage == 0 else self.send.at[stage - 1, rows]
        return pltpu.make_async_remote_copy(
            src_ref=src,
            dst_ref=self.recv.at[stage, rows],
            send_sem=self.ssem.at[k, stage],
            recv_sem=self.rsem.at[k, stage],
            device_id={"group": lax.axis_index("group") ^ bit},
            device_id_type=MESH,
        )

    def begin(self, k):
        self.copy(k, 0).start()

    def advance(self, k, stage):
        self.copy(k, stage - 1).wait_recv()
        if stage in (1, 3):
            s_own, s_got, o_own, o_got = self.factors(k, stage)

        def body(rows):
            at = pl.ds(k * self.size + rows.start, self.step)
            got = self.recv[stage - 1, at].astype(F32)
            if stage == 1:
                own = self.raw[at].astype(F32)
            else:
                own = self.acc[at]
            if stage in (1, 3):
                self.send[stage - 1, at] = (s_own * own + s_got * got).astype(BF16)
                self.acc[at] = o_own * own + o_got * got
            else:
                total = own + got
                self.acc[at] = total
                if stage == 2:
                    self.send[1, at] = total.astype(BF16)

        blocks(self.size, self.step, body)
        if stage < 4:
            self.copy(k, stage).start()

    def drain(self):
        for k in range(4):
            for stage in range(4):
                self.copy(k, stage).wait_send()


def level_factors(exponent, level):
    left = jnp.float32(1.0)
    for rnd in range(ROUNDS):
        left = left * jnp.where(exponent[rnd] == level, jnp.float32(1.0 - 2.0 * MIXES[rnd]), jnp.float32(1.0))
    return (1.0 + left) * 0.5, (1.0 - left) * 0.5


def step_kernel(
    with_far, exponent, inputs, teacher, weight, momentum, out_w, out_m,
    xc, wm, wc, tc, wm_acc, wm_send, wm_recv, part, flow_in, flow_out, cross_in, err,
    g_raw, g_acc, g_send, g_recv, fin, far_out, far_in,
    a2a_s, a2a_r, fwd_s, fwd_r, own_s, sib_s, sib_r, wm_ss, wm_rs, g0_ss, g0_rs, g1_ss, g1_rs,
    flow_s, flow_r, cross_s, cross_r, fin_l, fin_s, fin_r, far_s, far_r,
):
    group, f = lax.axis_index("group"), lax.axis_index("fsdp")
    z, c = f // 2, f % 2
    scale = D ** (-0.5)
    coef = {level: level_factors(exponent, level) for level in range(5)}

    barrier = pltpu.get_barrier_semaphore()

    def greet(i, carry):
        pl.semaphore_signal(
            barrier, inc=1, device_id={"fsdp": (f + i) % DEVS}, device_id_type=MESH
        )
        return carry

    lax.fori_loop(1, DEVS, greet, 0)
    bits = BITS["y"] + BITS["x"] + ((4,) if with_far else ())
    for bit in bits:
        pl.semaphore_signal(
            barrier, inc=1, device_id={"group": group ^ bit}, device_id_type=MESH
        )
    pl.semaphore_wait(barrier, DEVS - 1 + len(bits))

    def to_sibling(src, dst, s, r):
        return pltpu.make_async_remote_copy(
            src_ref=src, dst_ref=dst, send_sem=s, recv_sem=r,
            device_id={"fsdp": f ^ 1}, device_id_type=MESH,
        )

    def far_device(i, ahead):
        return (z + ahead) % CHIPS * 2 + i % 2

    def block(i, there):
        dev = far_device(i, i // 2 if there else CHIPS - i // 2)
        to = dev if there else f
        of = f if there else dev
        return dev, pltpu.make_async_remote_copy(
            src_ref=inputs.at[0, :, pl.ds(pl.multiple_of(to * ROWS, ROWS), ROWS)],
            dst_ref=xc.at[
                pl.ds(pl.multiple_of(of * TOK, TOK), TOK),
                pl.ds(pl.multiple_of((to % 2) * ROWS, ROWS), ROWS),
            ],
            send_sem=a2a_s.at[i],
            recv_sem=a2a_r.at[of],
            device_id={"fsdp": dev},
            device_id_type=MESH,
        )

    def send_block(i, carry):
        block(i, True)[1].start()
        return carry

    lax.fori_loop(2, DEVS, send_block, 0)

    mine = pl.ds(pl.multiple_of(c * HALF, HALF), HALF)
    other = pl.ds(pl.multiple_of((1 - c) * HALF, HALF), HALF)
    every = pl.ds(0, KV)
    w_rows = pl.ds(pl.multiple_of(c * ROWS, ROWS), ROWS)
    m_rows = pl.ds(pl.multiple_of(2 * ROWS + c * ROWS, ROWS), ROWS)
    t_rows = pl.ds(pl.multiple_of(c * TOK, TOK), TOK)
    x_rows = pl.ds(pl.multiple_of(f * TOK, TOK), TOK)
    x_cols = pl.ds(pl.multiple_of(z * 2 * ROWS, 2 * ROWS), 2 * ROWS)
    shared = (
        (weight, mine, other, wm, w_rows),
        (momentum, mine, other, wm, m_rows),
        (weight, every, every, wc, w_rows),
        (teacher, every, every, tc, t_rows),
        (inputs, x_cols, x_cols, xc, x_rows),
    )
    local = [
        pltpu.make_async_copy(src.at[0, :, keep], dst.at[rows], own_s.at[i])
        for i, (src, keep, _, dst, rows) in enumerate(shared)
    ]
    across = [
        to_sibling(src.at[0, :, give], dst.at[rows], sib_s.at[i], sib_r.at[i])
        for i, (src, _, give, dst, rows) in enumerate(shared)
    ]
    for i in range(5):
        local[i].start()
        across[i].start()

    def zeros(ref):
        ref[...] = jnp.zeros_like(ref)

    place = jnp.where(c == 0, z, CHIPS - 1 - z)
    pl.when(place == 0)(lambda: zeros(flow_in))
    pl.when(place == CHIPS - 1)(lambda: zeros(cross_in))

    for i in range(2):
        local[i].wait()
        across[i].wait()
    mix = Mix(wm, wm_acc, wm_send, wm_recv, wm_ss, wm_rs, coef, 64)
    for k in range(4):
        mix.begin(k)
    for stage in range(1, 5):
        for k in range(4):
            mix.advance(k, stage)
    mix.drain()

    def to_far(i):
        return pltpu.make_async_remote_copy(
            src_ref=far_out.at[i], dst_ref=far_in.at[i], send_sem=far_s.at[i], recv_sem=far_r.at[i],
            device_id={"group": group ^ 4}, device_id_type=MESH,
        )

    if with_far:

        def w_out(rows):
            for q in range(NQ):
                far_out[NQ + q, rows] = wm_acc[rows, q * QW : (q + 1) * QW].astype(BF16)

        blocks(2 * ROWS, 64, w_out)

    def item_of(q, core, t):
        return (q * 2 + core) * NT + t

    def share(chip):
        rows = pl.ds(pl.multiple_of(chip * ITEM, ITEM), ITEM)
        own = jnp.dot(xc[rows], wc[...], preferred_element_type=F32) * scale
        for core in range(2):
            for q in range(NQ):
                at = core * HALF + q * QW
                part[item_of(q, core, chip)] = own[:, at : at + QW]

    for i in range(2, 5):
        local[i].wait()
        across[i].wait()
    share(z)
    for core in range(2):
        for q in range(NQ):
            at = core * HALF + q * QW
            n = item_of(q, core, z)
            part[n] = part[n] - tc[:, at : at + QW].astype(F32)

    def forward(j, cols):
        at = (pl.ds(pl.multiple_of(j * TOK, TOK), TOK), pl.ds(pl.multiple_of(cols * ROWS, ROWS), ROWS))
        return to_sibling(xc.at[at], xc.at[at], fwd_s.at[j], fwd_r.at[j])

    def pass_on(ahead):
        for i in range(2):
            dev, arrival = block(2 * ahead + i, False)
            arrival.wait_recv()
            forward(dev, c).start()

    def settle(ahead):
        for i in range(2):
            dev = far_device(i, CHIPS - ahead)
            forward(dev, c).wait_send()
            forward(dev, 1 - c).wait_recv()
            block(2 * ahead + i, True)[1].wait_send()
        share((z + CHIPS - ahead) % CHIPS)

    def arrive(ahead, carry):
        pass_on(ahead)
        pl.when(ahead > 1)(lambda: settle(ahead - 1))
        return carry

    lax.fori_loop(1, CHIPS, arrive, 0)
    settle(CHIPS - 1)
    def hop(n):
        return pltpu.make_async_remote_copy(
            src_ref=flow_out.at[n], dst_ref=flow_in.at[n], send_sem=flow_s.at[n], recv_sem=flow_r.at[n],
            device_id={"fsdp": (f + DEVS + 2 - 4 * c) % DEVS}, device_id_type=MESH,
        )

    def cross(m, n):
        return to_sibling(flow_in.at[n], cross_in.at[m], cross_s.at[m], cross_r.at[m])

    sems = ((g0_ss, g0_rs), (g1_ss, g1_rs))
    mixes = [
        Mix(g_raw.at[q], g_acc.at[q], g_send.at[q], g_recv.at[q], *sems[q], coef, 256) for q in range(NQ)
    ]

    def grad(q):
        turned = err[q * NT : (q + 1) * NT].reshape(DEVS * TOK, QW).T
        for k in range(4):
            size = 2 * ROWS // 4
            got = jnp.dot(turned, xc[:, k * size : (k + 1) * size], preferred_element_type=F32)
            g_raw[q, k * size : (k + 1) * size] = (got * scale).T.astype(BF16)
            mixes[q].begin(k)

    def advance(q, stage):
        for k in range(4):
            mixes[q].advance(k, stage)

    def moved_of(q, rows):
        cols = slice(q * QW, (q + 1) * QW)
        return 0.9 * wm_acc[pl.ds(2 * ROWS + rows.start, 64), cols] + g_acc[q, rows]

    out_cols = [pl.ds(pl.multiple_of(c * HALF + q * QW, QW), QW) for q in range(NQ)]
    o_rows = pl.ds(pl.multiple_of((1 - c) * ROWS, ROWS), ROWS)

    def ends(q):
        copies = []
        for i, out in enumerate((out_w, out_m)):
            at = out.at[0, :, out_cols[q]]
            k = 2 * q + i
            copies.append(to_sibling(fin.at[k, o_rows], at, fin_s.at[k], fin_r.at[k]))
            copies.append(pltpu.make_async_copy(fin.at[k, w_rows], at, fin_l.at[k]))
        return copies

    def mixed(q):
        if with_far:

            def body(rows):
                far_out[q, rows] = moved_of(q, rows).astype(BF16)

            blocks(2 * ROWS, 64, body)
            to_far(q).start()
        else:

            def body(rows):
                moved = moved_of(q, rows)
                fin[2 * q + 1, rows] = moved.astype(BF16)
                fin[2 * q, rows] = (wm_acc[rows, q * QW : (q + 1) * QW] - 0.05 * moved).astype(BF16)

            blocks(2 * ROWS, 64, body)
            for copy in ends(q):
                copy.start()

    def finish(q):
        if with_far:
            own, far = coef[FAR_LEVEL]
            to_far(NQ + q).wait()
            to_far(q).wait()

            def body(rows):
                moved = own * moved_of(q, rows) + far * far_in[q, rows].astype(F32)
                kept = own * wm_acc[rows, q * QW : (q + 1) * QW] + far * far_in[NQ + q, rows].astype(F32)
                fin[2 * q + 1, rows] = moved.astype(BF16)
                fin[2 * q, rows] = (kept - 0.05 * moved).astype(BF16)

            blocks(2 * ROWS, 64, body)
            for copy in ends(q):
                copy.start()

    def own_index(n):
        return n // (2 * NT) * NT + n % NT

    lag = SKEW * jnp.maximum(CHIPS - 1 - 2 * place, 0) + MARGIN
    late = jnp.logical_and(place > LATE, place < CHIPS - 1 - LATE)

    def step(s, carry):
        @pl.when(s < NITEM)
        def _():
            @pl.when(place > 0)
            def _():
                hop(s).wait_recv()

            @pl.when(place < CHIPS - 1)
            def _():
                flow_out[s] = (part[s] + flow_in[s].astype(F32)).astype(BF16)
                hop(s).start()

            @pl.when(jnp.logical_and(place > 0, s // NT % 2 != c))
            def _():
                cross(own_index(s), s).start()

        n = s - lag

        @pl.when(jnp.logical_and(jnp.logical_and(n >= 0, n < NITEM), n // NT % 2 == c))
        def _():
            m = own_index(n)

            @pl.when(place < CHIPS - 1)
            def _():
                cross(m, n).wait_recv()

            err[m] = (part[n] + flow_in[n].astype(F32) + cross_in[m].astype(F32)).astype(BF16)

        @pl.when(jnp.logical_not(late))
        def _():
            pl.when(n == 2 * NT)(lambda: grad(0))
            for stage in range(1, 5):
                pl.when(n == 2 * NT + GAP * stage)(lambda stage=stage: advance(0, stage))

        return carry

    steps = max(NITEM, 2 * NT + 4 * GAP + 1)
    lax.fori_loop(0, steps + SKEW * (CHIPS - 1) + MARGIN, step, 0)

    pl.when(late)(lambda: grad(0))
    grad(1)
    if with_far:
        for q in range(NQ):
            to_far(NQ + q).start()

    pl.when(jnp.logical_not(late))(lambda: mixed(0))
    for stage in range(1, 5):
        pl.when(late)(lambda stage=stage: advance(0, stage))
        advance(1, stage)
    pl.when(late)(lambda: mixed(0))
    mixed(1)

    def sent(n, carry):
        pl.when(place < CHIPS - 1)(lambda: hop(n).wait_send())
        pl.when(jnp.logical_and(place > 0, n // NT % 2 != c))(lambda: cross(own_index(n), n).wait_send())
        return carry

    lax.fori_loop(0, NITEM, sent, 0)
    for q in range(NQ):
        mixes[q].drain()
    for q in range(NQ):
        finish(q)
    for q in range(NQ):
        for copy in ends(q):
            copy.wait()


def step_call(with_far, exponent, inputs, teacher, weight, momentum):
    dma = lambda *n: pltpu.SemaphoreType.DMA(n)
    anywhere = pl.BlockSpec(memory_space=pl.ANY)
    shape = jax.ShapeDtypeStruct((1, ROWS, KV), BF16)
    rows = 2 * ROWS
    far = 2 * NQ
    return pl.pallas_call(
        functools.partial(step_kernel, with_far),
        name="step_far" if with_far else "step_near",
        out_shape=(shape, shape),
        in_specs=[pl.BlockSpec(memory_space=pltpu.SMEM)] + [anywhere] * 4,
        out_specs=(anywhere, anywhere),
        scratch_shapes=[
            pltpu.VMEM((DEVS * TOK, rows), BF16),
            pltpu.VMEM((2 * rows, HALF), BF16),
            pltpu.VMEM((rows, KV), BF16),
            pltpu.VMEM((2 * TOK, KV), BF16),
            pltpu.VMEM((2 * rows, HALF), F32),
            pltpu.VMEM((3, 2 * rows, HALF), BF16),
            pltpu.VMEM((4, 2 * rows, HALF), BF16),
            pltpu.VMEM((NITEM, ITEM, QW), F32),
            pltpu.VMEM((NITEM, ITEM, QW), BF16),
            pltpu.VMEM((NITEM, ITEM, QW), BF16),
            pltpu.VMEM((NOWN, ITEM, QW), BF16),
            pltpu.VMEM((NOWN, ITEM, QW), BF16),
            pltpu.VMEM((NQ, rows, QW), BF16),
            pltpu.VMEM((NQ, rows, QW), F32),
            pltpu.VMEM((NQ, 3, rows, QW), BF16),
            pltpu.VMEM((NQ, 4, rows, QW), BF16),
            pltpu.VMEM((2 * NQ, rows, QW), BF16),
            pltpu.VMEM((far, rows, QW), BF16),
            pltpu.VMEM((far, rows, QW), BF16),
            dma(DEVS), dma(DEVS), dma(DEVS), dma(DEVS),
            dma(5), dma(5), dma(5),
            dma(4, 4), dma(4, 4), dma(4, 4), dma(4, 4), dma(4, 4), dma(4, 4),
            dma(NITEM), dma(NITEM), dma(NOWN), dma(NOWN),
            dma(2 * NQ), dma(2 * NQ), dma(2 * NQ),
            dma(far), dma(far),
        ],
        compiler_params=pltpu.CompilerParams(
            collective_id=int(with_far), has_side_effects=True, vmem_limit_bytes=56 * 2**20
        ),
    )(exponent, inputs, teacher, weight, momentum)


def per_device(inputs, teacher, weight, momentum, exponent):
    return lax.cond(
        jnp.any(exponent == FAR_LEVEL),
        lambda *args: tuple(step_call(True, *args)),
        lambda *args: tuple(step_call(False, *args)),
        exponent, inputs, teacher, weight, momentum,
    )


def solution(mesh):
    return jax.shard_map(
        per_device,
        mesh=mesh,
        in_specs=(
            P("group", "fsdp", None),
            P("group", "fsdp", None),
            P("group", "fsdp", None),
            P("group", "fsdp", None),
            P(),
        ),
        out_specs=(P("group", "fsdp", None), P("group", "fsdp", None)),
        check_vma=False,
    )
```

```python
import functools

import jax
import jax.numpy as jnp
from jax import lax
from jax.experimental import pallas as pl
from jax.experimental.pallas import tpu as pltpu
from jax.sharding import PartitionSpec as P

D = 8192
KV = 512
ROUNDS = 4
MIXES = (0.5, 0.4, 0.3, 0.2)
MESH = pl.DeviceIdType.MESH
F32 = jnp.float32
BF16 = jnp.bfloat16

CHIPS = 8
DEVS = 16
TOK = 128
ROWS = 512
HALF = KV // 2
QW = 128
ITEM = 256
NT = DEVS * TOK // ITEM
NQ = HALF // QW
NOWN = NT * NQ
NITEM = 2 * NOWN
SKEW = 4
MARGIN = 2
LATE = 1
GAP = 4

ORDERS = (("y", 0), ("y", 1), ("x", 0), ("x", 1))
BITS = {"y": (1, 3), "x": (8, 24)}
LEVELS = {"y": (0, 1), "x": (3, 4)}
FAR_LEVEL = 2
NEAR, FAR_WHOLE, FAR_HALF = range(3)
SHARE_LEVELS = (0, 1, 3, 4)
PIECE = 256


def blocks(rows, step, body):
    def one(i, carry):
        body(pl.ds(pl.multiple_of(i * step, step), step))
        return carry

    lax.fori_loop(0, rows // step, one, 0)


class Mix:
    def __init__(self, raw, acc, send, recv, ssem, rsem, coef, step):
        self.raw, self.acc, self.send, self.recv = raw, acc, send, recv
        self.ssem, self.rsem, self.coef, self.step = ssem, rsem, coef, step
        self.size = raw.shape[0] // 4

    def axis_of(self, k, stage):
        first, order = ORDERS[k]
        axis = first if stage < 2 else ("x" if first == "y" else "y")
        return axis, order

    def factors(self, k, stage):
        axis, order = self.axis_of(k, stage)
        (a0, b0), (a1, b1) = (self.coef[level] for level in LEVELS[axis])
        if order == 0:
            return b0 * b1, a0 * b1, a0 * a1, b0 * a1
        return b0 * a1, a0 * b1, a0 * a1, b0 * b1

    def copy(self, k, stage):
        axis, order = self.axis_of(k, stage)
        bit = BITS[axis][order if stage % 2 == 0 else 1 - order]
        rows = pl.ds(k * self.size, self.size)
        src = self.raw.at[rows] if stage == 0 else self.send.at[stage - 1, rows]
        return pltpu.make_async_remote_copy(
            src_ref=src,
            dst_ref=self.recv.at[stage, rows],
            send_sem=self.ssem.at[k, stage],
            recv_sem=self.rsem.at[k, stage],
            device_id={"group": lax.axis_index("group") ^ bit},
            device_id_type=MESH,
        )

    def begin(self, k):
        self.copy(k, 0).start()

    def advance(self, k, stage):
        self.copy(k, stage - 1).wait_recv()
        if stage in (1, 3):
            s_own, s_got, o_own, o_got = self.factors(k, stage)

        def body(rows):
            at = pl.ds(k * self.size + rows.start, self.step)
            got = self.recv[stage - 1, at].astype(F32)
            if stage == 1:
                own = self.raw[at].astype(F32)
            else:
                own = self.acc[at]
            if stage in (1, 3):
                self.send[stage - 1, at] = (s_own * own + s_got * got).astype(BF16)
                self.acc[at] = o_own * own + o_got * got
            else:
                total = own + got
                self.acc[at] = total
                if stage == 2:
                    self.send[1, at] = total.astype(BF16)

        blocks(self.size, self.step, body)
        if stage < 4:
            self.copy(k, stage).start()

    def drain(self):
        for k in range(4):
            for stage in range(4):
                self.copy(k, stage).wait_send()


def level_factors(exponent, level):
    left = jnp.float32(1.0)
    for rnd in range(ROUNDS):
        left = left * jnp.where(exponent[rnd] == level, jnp.float32(1.0 - 2.0 * MIXES[rnd]), jnp.float32(1.0))
    return (1.0 + left) * 0.5, (1.0 - left) * 0.5


def step_kernel(
    mode, exponent, inputs, teacher, weight, momentum, out_w, out_m,
    xc, wm, wc, tc, wm_acc, wm_send, wm_recv, part, flow_in, flow_out, cross_in, err,
    g_raw, g_acc, g_send, g_recv, fin, far_out, far_in, share_in,
    a2a_s, a2a_r, fwd_s, fwd_r, own_s, sib_s, sib_r, wm_ss, wm_rs, g0_ss, g0_rs, g1_ss, g1_rs,
    flow_s, flow_r, cross_s, cross_r, fin_l, fin_s, fin_r, far_s, far_r, share_s, share_r,
):
    group, f = lax.axis_index("group"), lax.axis_index("fsdp")
    z, c = f // 2, f % 2
    scale = D ** (-0.5)
    coef = {level: level_factors(exponent, level) for level in range(5)}

    barrier = pltpu.get_barrier_semaphore()

    def greet(i, carry):
        pl.semaphore_signal(
            barrier, inc=1, device_id={"fsdp": (f + i) % DEVS}, device_id_type=MESH
        )
        return carry

    lax.fori_loop(1, DEVS, greet, 0)
    with_far = mode != NEAR
    bits = BITS["y"] + BITS["x"] + ((4,) if with_far else ()) + ((2, 16) if mode == FAR_HALF else ())
    for bit in bits:
        pl.semaphore_signal(
            barrier, inc=1, device_id={"group": group ^ bit}, device_id_type=MESH
        )
    pl.semaphore_wait(barrier, DEVS - 1 + len(bits))

    def to_sibling(src, dst, s, r):
        return pltpu.make_async_remote_copy(
            src_ref=src, dst_ref=dst, send_sem=s, recv_sem=r,
            device_id={"fsdp": f ^ 1}, device_id_type=MESH,
        )

    def far_device(i, ahead):
        return (z + ahead) % CHIPS * 2 + i % 2

    def block(i, there):
        dev = far_device(i, i // 2 if there else CHIPS - i // 2)
        to = dev if there else f
        of = f if there else dev
        return dev, pltpu.make_async_remote_copy(
            src_ref=inputs.at[0, :, pl.ds(pl.multiple_of(to * ROWS, ROWS), ROWS)],
            dst_ref=xc.at[
                pl.ds(pl.multiple_of(of * TOK, TOK), TOK),
                pl.ds(pl.multiple_of((to % 2) * ROWS, ROWS), ROWS),
            ],
            send_sem=a2a_s.at[i],
            recv_sem=a2a_r.at[of],
            device_id={"fsdp": dev},
            device_id_type=MESH,
        )

    def send_block(i, carry):
        block(i, True)[1].start()
        return carry

    lax.fori_loop(2, DEVS, send_block, 0)

    mine = pl.ds(pl.multiple_of(c * HALF, HALF), HALF)
    other = pl.ds(pl.multiple_of((1 - c) * HALF, HALF), HALF)
    every = pl.ds(0, KV)
    w_rows = pl.ds(pl.multiple_of(c * ROWS, ROWS), ROWS)
    m_rows = pl.ds(pl.multiple_of(2 * ROWS + c * ROWS, ROWS), ROWS)
    t_rows = pl.ds(pl.multiple_of(c * TOK, TOK), TOK)
    x_rows = pl.ds(pl.multiple_of(f * TOK, TOK), TOK)
    x_cols = pl.ds(pl.multiple_of(z * 2 * ROWS, 2 * ROWS), 2 * ROWS)
    shared = (
        (weight, mine, other, wm, w_rows),
        (momentum, mine, other, wm, m_rows),
        (weight, every, every, wc, w_rows),
        (teacher, every, every, tc, t_rows),
        (inputs, x_cols, x_cols, xc, x_rows),
    )
    local = [
        pltpu.make_async_copy(src.at[0, :, keep], dst.at[rows], own_s.at[i])
        for i, (src, keep, _, dst, rows) in enumerate(shared)
    ]
    across = [
        to_sibling(src.at[0, :, give], dst.at[rows], sib_s.at[i], sib_r.at[i])
        for i, (src, _, give, dst, rows) in enumerate(shared)
    ]
    for i in range(5):
        local[i].start()
        across[i].start()

    def zeros(ref):
        ref[...] = jnp.zeros_like(ref)

    place = jnp.where(c == 0, z, CHIPS - 1 - z)
    pl.when(place == 0)(lambda: zeros(flow_in))
    pl.when(place == CHIPS - 1)(lambda: zeros(cross_in))

    for i in range(2):
        local[i].wait()
        across[i].wait()
    mix = Mix(wm, wm_acc, wm_send, wm_recv, wm_ss, wm_rs, coef, 64)
    for k in range(4):
        mix.begin(k)
    for stage in range(1, 5):
        for k in range(4):
            mix.advance(k, stage)
    mix.drain()

    half = (group + group // 2 + group // 8 + group // 16) % 2
    first_row = half * ROWS if mode == FAR_HALF else 0
    pieces = (ROWS if mode == FAR_HALF else 2 * ROWS) // PIECE

    def to_far(i, p):
        rows = pl.ds(pl.multiple_of(first_row + p * PIECE, PIECE), PIECE)
        return pltpu.make_async_remote_copy(
            src_ref=far_out.at[i, rows], dst_ref=far_in.at[i, rows],
            send_sem=far_s.at[i, p], recv_sem=far_r.at[i, p],
            device_id={"group": group ^ 4}, device_id_type=MESH,
        )

    def send_far(i):
        for p in range(pieces):
            to_far(i, p).start()

    def to_share(i, p, k):
        rows = pl.ds(pl.multiple_of(first_row + p * PIECE, PIECE), PIECE)
        return pltpu.make_async_remote_copy(
            src_ref=far_in.at[i, rows], dst_ref=share_in.at[k, i, pl.ds(p * PIECE, PIECE)],
            send_sem=share_s.at[k, i, p], recv_sem=share_r.at[k, i, p],
            device_id={"group": group ^ (1 << SHARE_LEVELS[k])}, device_id_type=MESH,
        )

    def hand_on(i):
        for p in range(pieces):
            to_far(i, p).wait_recv()
            if mode == FAR_HALF:
                for k in range(len(SHARE_LEVELS)):
                    to_share(i, p, k).start()

    if with_far:

        def w_out(rows):
            for q in range(NQ):
                far_out[NQ + q, rows] = wm_acc[rows, q * QW : (q + 1) * QW].astype(BF16)

        blocks(2 * ROWS, 64, w_out)

    def item_of(q, core, t):
        return (q * 2 + core) * NT + t

    def share(chip):
        rows = pl.ds(pl.multiple_of(chip * ITEM, ITEM), ITEM)
        own = jnp.dot(xc[rows], wc[...], preferred_element_type=F32) * scale
        for core in range(2):
            for q in range(NQ):
                at = core * HALF + q * QW
                part[item_of(q, core, chip)] = own[:, at : at + QW]

    for i in range(2, 5):
        local[i].wait()
        across[i].wait()
    share(z)
    for core in range(2):
        for q in range(NQ):
            at = core * HALF + q * QW
            n = item_of(q, core, z)
            part[n] = part[n] - tc[:, at : at + QW].astype(F32)

    def forward(j, cols):
        at = (pl.ds(pl.multiple_of(j * TOK, TOK), TOK), pl.ds(pl.multiple_of(cols * ROWS, ROWS), ROWS))
        return to_sibling(xc.at[at], xc.at[at], fwd_s.at[j], fwd_r.at[j])

    def pass_on(ahead):
        for i in range(2):
            dev, arrival = block(2 * ahead + i, False)
            arrival.wait_recv()
            forward(dev, c).start()

    def settle(ahead):
        for i in range(2):
            dev = far_device(i, CHIPS - ahead)
            forward(dev, c).wait_send()
            forward(dev, 1 - c).wait_recv()
            block(2 * ahead + i, True)[1].wait_send()
        share((z + CHIPS - ahead) % CHIPS)

    def arrive(ahead, carry):
        pass_on(ahead)
        pl.when(ahead > 1)(lambda: settle(ahead - 1))
        return carry

    lax.fori_loop(1, CHIPS, arrive, 0)
    settle(CHIPS - 1)
    if with_far:
        for q in range(NQ):
            send_far(NQ + q)

    def hop(n):
        return pltpu.make_async_remote_copy(
            src_ref=flow_out.at[n], dst_ref=flow_in.at[n], send_sem=flow_s.at[n], recv_sem=flow_r.at[n],
            device_id={"fsdp": (f + DEVS + 2 - 4 * c) % DEVS}, device_id_type=MESH,
        )

    def cross(m, n):
        return to_sibling(flow_in.at[n], cross_in.at[m], cross_s.at[m], cross_r.at[m])

    sems = ((g0_ss, g0_rs), (g1_ss, g1_rs))
    mixes = [
        Mix(g_raw.at[q], g_acc.at[q], g_send.at[q], g_recv.at[q], *sems[q], coef, 256) for q in range(NQ)
    ]

    def grad(q):
        turned = err[q * NT : (q + 1) * NT].reshape(DEVS * TOK, QW).T
        for k in range(4):
            size = 2 * ROWS // 4
            got = jnp.dot(turned, xc[:, k * size : (k + 1) * size], preferred_element_type=F32)
            g_raw[q, k * size : (k + 1) * size] = (got * scale).T.astype(BF16)
            mixes[q].begin(k)

    def advance(q, stage):
        for k in range(4):
            mixes[q].advance(k, stage)

    def moved_of(q, rows):
        cols = slice(q * QW, (q + 1) * QW)
        return 0.9 * wm_acc[pl.ds(2 * ROWS + rows.start, 64), cols] + g_acc[q, rows]

    out_cols = [pl.ds(pl.multiple_of(c * HALF + q * QW, QW), QW) for q in range(NQ)]
    o_rows = pl.ds(pl.multiple_of((1 - c) * ROWS, ROWS), ROWS)

    def ends(q):
        copies = []
        for i, out in enumerate((out_w, out_m)):
            at = out.at[0, :, out_cols[q]]
            k = 2 * q + i
            copies.append(to_sibling(fin.at[k, o_rows], at, fin_s.at[k], fin_r.at[k]))
            copies.append(pltpu.make_async_copy(fin.at[k, w_rows], at, fin_l.at[k]))
        return copies

    def mixed(q):
        if with_far:

            def body(rows):
                far_out[q, rows] = moved_of(q, rows).astype(BF16)

            blocks(2 * ROWS, 64, body)
            send_far(q)
        else:

            def body(rows):
                moved = moved_of(q, rows)
                fin[2 * q + 1, rows] = moved.astype(BF16)
                fin[2 * q, rows] = (wm_acc[rows, q * QW : (q + 1) * QW] - 0.05 * moved).astype(BF16)

            blocks(2 * ROWS, 64, body)
            for copy in ends(q):
                copy.start()

    def finish(q):
        if with_far:
            own, far = coef[FAR_LEVEL]
            if mode == FAR_HALF:
                for i in (NQ + q, q):
                    for p in range(pieces):
                        for k in range(len(SHARE_LEVELS)):
                            to_share(i, p, k).wait_recv()

            def shared_far(i, at):
                got = share_in[0, i, at]
                for k in range(1, len(SHARE_LEVELS)):
                    got = jnp.where(exponent[0] == SHARE_LEVELS[k], share_in[k, i, at], got)
                return got.astype(F32)

            def end(rows, far_of):
                moved = own * moved_of(q, rows) + far * far_of(q)
                kept = own * wm_acc[rows, q * QW : (q + 1) * QW] + far * far_of(NQ + q)
                fin[2 * q + 1, rows] = moved.astype(BF16)
                fin[2 * q, rows] = (kept - 0.05 * moved).astype(BF16)

            def direct(at):
                rows = pl.ds(pl.multiple_of(first_row + at.start, 64), 64)
                end(rows, lambda i: far_in[i, rows].astype(F32))

            def handed(at):
                rows = pl.ds(pl.multiple_of((1 - half) * ROWS + at.start, 64), 64)
                end(rows, lambda i: shared_far(i, at))

            blocks(pieces * PIECE, 64, direct)
            if mode == FAR_HALF:
                blocks(ROWS, 64, handed)
            for copy in ends(q):
                copy.start()

    def own_index(n):
        return n // (2 * NT) * NT + n % NT

    lag = SKEW * jnp.maximum(CHIPS - 1 - 2 * place, 0) + MARGIN
    late = jnp.logical_and(place > LATE, place < CHIPS - 1 - LATE)

    def step(s, carry):
        @pl.when(s < NITEM)
        def _():
            @pl.when(place > 0)
            def _():
                hop(s).wait_recv()

            @pl.when(place < CHIPS - 1)
            def _():
                flow_out[s] = (part[s] + flow_in[s].astype(F32)).astype(BF16)
                hop(s).start()

            @pl.when(jnp.logical_and(place > 0, s // NT % 2 != c))
            def _():
                cross(own_index(s), s).start()

        n = s - lag

        @pl.when(jnp.logical_and(jnp.logical_and(n >= 0, n < NITEM), n // NT % 2 == c))
        def _():
            m = own_index(n)

            @pl.when(place < CHIPS - 1)
            def _():
                cross(m, n).wait_recv()

            err[m] = (part[n] + flow_in[n].astype(F32) + cross_in[m].astype(F32)).astype(BF16)

        @pl.when(jnp.logical_not(late))
        def _():
            pl.when(n == 2 * NT)(lambda: grad(0))
            for stage in range(1, 5):
                pl.when(n == 2 * NT + GAP * stage)(lambda stage=stage: advance(0, stage))

        return carry

    steps = max(NITEM, 2 * NT + 4 * GAP + 1)
    lax.fori_loop(0, steps + SKEW * (CHIPS - 1) + MARGIN, step, 0)

    pl.when(late)(lambda: grad(0))
    grad(1)
    pl.when(jnp.logical_not(late))(lambda: mixed(0))
    for stage in range(1, 5):
        pl.when(late)(lambda stage=stage: advance(0, stage))
        advance(1, stage)
    pl.when(late)(lambda: mixed(0))
    mixed(1)

    def sent(n, carry):
        pl.when(place < CHIPS - 1)(lambda: hop(n).wait_send())
        pl.when(jnp.logical_and(place > 0, n // NT % 2 != c))(lambda: cross(own_index(n), n).wait_send())
        return carry

    lax.fori_loop(0, NITEM, sent, 0)
    for q in range(NQ):
        mixes[q].drain()
    if with_far:
        for q in range(NQ):
            hand_on(NQ + q)
        for q in range(NQ):
            hand_on(q)
    for q in range(NQ):
        finish(q)
    if with_far:
        for i in range(2 * NQ):
            for p in range(pieces):
                to_far(i, p).wait_send()
                if mode == FAR_HALF:
                    for k in range(len(SHARE_LEVELS)):
                        to_share(i, p, k).wait_send()
    for q in range(NQ):
        for copy in ends(q):
            copy.wait()


def step_call(mode, exponent, inputs, teacher, weight, momentum):
    dma = lambda *n: pltpu.SemaphoreType.DMA(n)
    anywhere = pl.BlockSpec(memory_space=pl.ANY)
    shape = jax.ShapeDtypeStruct((1, ROWS, KV), BF16)
    rows = 2 * ROWS
    far = 2 * NQ
    return pl.pallas_call(
        functools.partial(step_kernel, mode),
        name=("step_near", "step_far_whole", "step_far_half")[mode],
        out_shape=(shape, shape),
        in_specs=[pl.BlockSpec(memory_space=pltpu.SMEM)] + [anywhere] * 4,
        out_specs=(anywhere, anywhere),
        scratch_shapes=[
            pltpu.VMEM((DEVS * TOK, rows), BF16),
            pltpu.VMEM((2 * rows, HALF), BF16),
            pltpu.VMEM((rows, KV), BF16),
            pltpu.VMEM((2 * TOK, KV), BF16),
            pltpu.VMEM((2 * rows, HALF), F32),
            pltpu.VMEM((3, 2 * rows, HALF), BF16),
            pltpu.VMEM((4, 2 * rows, HALF), BF16),
            pltpu.VMEM((NITEM, ITEM, QW), F32),
            pltpu.VMEM((NITEM, ITEM, QW), BF16),
            pltpu.VMEM((NITEM, ITEM, QW), BF16),
            pltpu.VMEM((NOWN, ITEM, QW), BF16),
            pltpu.VMEM((NOWN, ITEM, QW), BF16),
            pltpu.VMEM((NQ, rows, QW), BF16),
            pltpu.VMEM((NQ, rows, QW), F32),
            pltpu.VMEM((NQ, 3, rows, QW), BF16),
            pltpu.VMEM((NQ, 4, rows, QW), BF16),
            pltpu.VMEM((2 * NQ, rows, QW), BF16),
            pltpu.VMEM((far, rows, QW), BF16),
            pltpu.VMEM((far, rows, QW), BF16),
            pltpu.VMEM((len(SHARE_LEVELS), far, ROWS, QW), BF16),
            dma(DEVS), dma(DEVS), dma(DEVS), dma(DEVS),
            dma(5), dma(5), dma(5),
            dma(4, 4), dma(4, 4), dma(4, 4), dma(4, 4), dma(4, 4), dma(4, 4),
            dma(NITEM), dma(NITEM), dma(NOWN), dma(NOWN),
            dma(2 * NQ), dma(2 * NQ), dma(2 * NQ),
            dma(far, rows // PIECE), dma(far, rows // PIECE),
            dma(len(SHARE_LEVELS), far, ROWS // PIECE), dma(len(SHARE_LEVELS), far, ROWS // PIECE),
        ],
        compiler_params=pltpu.CompilerParams(
            collective_id=mode, has_side_effects=True, vmem_limit_bytes=56 * 2**20
        ),
    )(exponent, inputs, teacher, weight, momentum)


def per_device(inputs, teacher, weight, momentum, exponent):
    far = jnp.where(exponent[0] == FAR_LEVEL, FAR_WHOLE, FAR_HALF)
    return lax.switch(
        jnp.where(jnp.any(exponent == FAR_LEVEL), far, NEAR),
        [lambda *args, mode=mode: tuple(step_call(mode, *args)) for mode in (NEAR, FAR_WHOLE, FAR_HALF)],
        exponent, inputs, teacher, weight, momentum,
    )


def solution(mesh):
    return jax.shard_map(
        per_device,
        mesh=mesh,
        in_specs=(
            P("group", "fsdp", None),
            P("group", "fsdp", None),
            P("group", "fsdp", None),
            P("group", "fsdp", None),
            P(),
        ),
        out_specs=(P("group", "fsdp", None), P("group", "fsdp", None)),
        check_vma=False,
    )
```

```python
import functools

import jax
import jax.numpy as jnp
from jax import lax
from jax.experimental import pallas as pl
from jax.experimental.pallas import tpu as pltpu
from jax.sharding import PartitionSpec as P

D = 8192
KV = 512
ROUNDS = 4
MIXES = (0.5, 0.4, 0.3, 0.2)
MESH = pl.DeviceIdType.MESH
F32 = jnp.float32
BF16 = jnp.bfloat16

CHIPS = 8
DEVS = 16
TOK = 128
ROWS = 512
HALF = KV // 2
QW = 128
ITEM = 256
NT = DEVS * TOK // ITEM
NQ = HALF // QW
NOWN = NT * NQ
NITEM = 2 * NOWN
SKEW = 4
MARGIN = 2
LATE = 1
GAP = 4

ORDERS = (("y", 0), ("y", 1), ("x", 0), ("x", 1))
BITS = {"y": (1, 3), "x": (8, 24)}
LEVELS = {"y": (0, 1), "x": (3, 4)}
FAR_LEVEL = 2
NEAR, FAR_WHOLE, FAR_HALF = range(3)
SHARE_LEVELS = (0, 1, 3, 4)
PIECE = 256


def blocks(rows, step, body):
    def one(i, carry):
        body(pl.ds(pl.multiple_of(i * step, step), step))
        return carry

    lax.fori_loop(0, rows // step, one, 0)


class Mix:
    def __init__(self, raw, acc, send, recv, ssem, rsem, coef, step):
        self.raw, self.acc, self.send, self.recv = raw, acc, send, recv
        self.ssem, self.rsem, self.coef, self.step = ssem, rsem, coef, step
        self.size = raw.shape[0] // 4

    def axis_of(self, k, stage):
        first, order = ORDERS[k]
        axis = first if stage < 2 else ("x" if first == "y" else "y")
        return axis, order

    def factors(self, k, stage):
        axis, order = self.axis_of(k, stage)
        (a0, b0), (a1, b1) = (self.coef[level] for level in LEVELS[axis])
        if order == 0:
            return b0 * b1, a0 * b1, a0 * a1, b0 * a1
        return b0 * a1, a0 * b1, a0 * a1, b0 * b1

    def copy(self, k, stage):
        axis, order = self.axis_of(k, stage)
        bit = BITS[axis][order if stage % 2 == 0 else 1 - order]
        rows = pl.ds(k * self.size, self.size)
        src = self.raw.at[rows] if stage == 0 else self.send.at[stage - 1, rows]
        return pltpu.make_async_remote_copy(
            src_ref=src,
            dst_ref=self.recv.at[stage, rows],
            send_sem=self.ssem.at[k, stage],
            recv_sem=self.rsem.at[k, stage],
            device_id={"group": lax.axis_index("group") ^ bit},
            device_id_type=MESH,
        )

    def begin(self, k):
        self.copy(k, 0).start()

    def advance(self, k, stage):
        self.copy(k, stage - 1).wait_recv()
        if stage in (1, 3):
            s_own, s_got, o_own, o_got = self.factors(k, stage)

        def body(rows):
            at = pl.ds(k * self.size + rows.start, self.step)
            got = self.recv[stage - 1, at].astype(F32)
            if stage == 1:
                own = self.raw[at].astype(F32)
            else:
                own = self.acc[at]
            if stage in (1, 3):
                self.send[stage - 1, at] = (s_own * own + s_got * got).astype(BF16)
                self.acc[at] = o_own * own + o_got * got
            else:
                total = own + got
                self.acc[at] = total
                if stage == 2:
                    self.send[1, at] = total.astype(BF16)

        blocks(self.size, self.step, body)
        if stage < 4:
            self.copy(k, stage).start()

    def drain(self):
        for k in range(4):
            for stage in range(4):
                self.copy(k, stage).wait_send()


def level_factors(exponent, level):
    left = jnp.float32(1.0)
    for rnd in range(ROUNDS):
        left = left * jnp.where(exponent[rnd] == level, jnp.float32(1.0 - 2.0 * MIXES[rnd]), jnp.float32(1.0))
    return (1.0 + left) * 0.5, (1.0 - left) * 0.5


def step_kernel(
    mode, exponent, inputs, teacher, weight, momentum, out_w, out_m,
    xc, wm, wc, tc, wm_acc, wm_send, wm_recv, part, flow_in, flow_out, cross_in, err,
    g_raw, g_acc, g_send, g_recv, fin, far_out, far_in, share_in,
    a2a_s, a2a_r, fwd_s, fwd_r, own_s, sib_s, sib_r, wm_ss, wm_rs, g0_ss, g0_rs, g1_ss, g1_rs,
    flow_s, flow_r, cross_s, cross_r, fin_l, fin_s, fin_r, far_s, far_r, share_s, share_r,
):
    group, f = lax.axis_index("group"), lax.axis_index("fsdp")
    z, c = f // 2, f % 2
    scale = D ** (-0.5)
    coef = {level: level_factors(exponent, level) for level in range(5)}

    barrier = pltpu.get_barrier_semaphore()

    def greet(i, carry):
        pl.semaphore_signal(
            barrier, inc=1, device_id={"fsdp": (f + i) % DEVS}, device_id_type=MESH
        )
        return carry

    lax.fori_loop(1, DEVS, greet, 0)
    with_far = mode != NEAR
    bits = BITS["y"] + BITS["x"] + ((4,) if with_far else ()) + ((2, 16) if mode == FAR_HALF else ())
    for bit in bits:
        pl.semaphore_signal(
            barrier, inc=1, device_id={"group": group ^ bit}, device_id_type=MESH
        )
    pl.semaphore_wait(barrier, DEVS - 1 + len(bits))

    def to_sibling(src, dst, s, r):
        return pltpu.make_async_remote_copy(
            src_ref=src, dst_ref=dst, send_sem=s, recv_sem=r,
            device_id={"fsdp": f ^ 1}, device_id_type=MESH,
        )

    def far_device(i, ahead):
        return (z + ahead) % CHIPS * 2 + i % 2

    def block(i, there):
        dev = far_device(i, i // 2 if there else CHIPS - i // 2)
        to = dev if there else f
        of = f if there else dev
        return dev, pltpu.make_async_remote_copy(
            src_ref=inputs.at[0, :, pl.ds(pl.multiple_of(to * ROWS, ROWS), ROWS)],
            dst_ref=xc.at[
                pl.ds(pl.multiple_of(of * TOK, TOK), TOK),
                pl.ds(pl.multiple_of((to % 2) * ROWS, ROWS), ROWS),
            ],
            send_sem=a2a_s.at[i],
            recv_sem=a2a_r.at[of],
            device_id={"fsdp": dev},
            device_id_type=MESH,
        )

    def send_block(i, carry):
        block(i, True)[1].start()
        return carry

    lax.fori_loop(2, DEVS, send_block, 0)

    mine = pl.ds(pl.multiple_of(c * HALF, HALF), HALF)
    other = pl.ds(pl.multiple_of((1 - c) * HALF, HALF), HALF)
    every = pl.ds(0, KV)
    w_rows = pl.ds(pl.multiple_of(c * ROWS, ROWS), ROWS)
    m_rows = pl.ds(pl.multiple_of(2 * ROWS + c * ROWS, ROWS), ROWS)
    t_rows = pl.ds(pl.multiple_of(c * TOK, TOK), TOK)
    x_rows = pl.ds(pl.multiple_of(f * TOK, TOK), TOK)
    x_cols = pl.ds(pl.multiple_of(z * 2 * ROWS, 2 * ROWS), 2 * ROWS)
    shared = (
        (weight, mine, other, wm, w_rows),
        (momentum, mine, other, wm, m_rows),
        (weight, every, every, wc, w_rows),
        (teacher, every, every, tc, t_rows),
        (inputs, x_cols, x_cols, xc, x_rows),
    )
    local = [
        pltpu.make_async_copy(src.at[0, :, keep], dst.at[rows], own_s.at[i])
        for i, (src, keep, _, dst, rows) in enumerate(shared)
    ]
    across = [
        to_sibling(src.at[0, :, give], dst.at[rows], sib_s.at[i], sib_r.at[i])
        for i, (src, _, give, dst, rows) in enumerate(shared)
    ]
    for i in range(5):
        local[i].start()
        across[i].start()

    def zeros(ref):
        ref[...] = jnp.zeros_like(ref)

    place = jnp.where(c == 0, z, CHIPS - 1 - z)
    pl.when(place == 0)(lambda: zeros(flow_in))
    pl.when(place == CHIPS - 1)(lambda: zeros(cross_in))

    for i in range(2):
        local[i].wait()
        across[i].wait()
    mix = Mix(wm, wm_acc, wm_send, wm_recv, wm_ss, wm_rs, coef, 64)
    for k in range(4):
        mix.begin(k)
    for stage in range(1, 5):
        for k in range(4):
            mix.advance(k, stage)
    mix.drain()

    half = (group + group // 2 + group // 8 + group // 16) % 2
    first_row = half * ROWS if mode == FAR_HALF else 0
    pieces = (ROWS if mode == FAR_HALF else 2 * ROWS) // PIECE

    def to_far(i, p):
        rows = pl.ds(pl.multiple_of(first_row + p * PIECE, PIECE), PIECE)
        return pltpu.make_async_remote_copy(
            src_ref=far_out.at[i, rows], dst_ref=far_in.at[i, rows],
            send_sem=far_s.at[i, p], recv_sem=far_r.at[i, p],
            device_id={"group": group ^ 4}, device_id_type=MESH,
        )

    def send_far(i):
        for p in range(pieces):
            to_far(i, p).start()

    def to_share(i, p, k):
        rows = pl.ds(pl.multiple_of(first_row + p * PIECE, PIECE), PIECE)
        return pltpu.make_async_remote_copy(
            src_ref=far_in.at[i, rows], dst_ref=share_in.at[k, i, pl.ds(p * PIECE, PIECE)],
            send_sem=share_s.at[k, i, p], recv_sem=share_r.at[k, i, p],
            device_id={"group": group ^ (1 << SHARE_LEVELS[k])}, device_id_type=MESH,
        )

    def hand_on(i):
        for p in range(pieces):
            to_far(i, p).wait_recv()
            if mode == FAR_HALF:
                for k in range(len(SHARE_LEVELS)):
                    to_share(i, p, k).start()

    if with_far:

        def w_out(rows):
            for q in range(NQ):
                far_out[NQ + q, rows] = wm_acc[rows, q * QW : (q + 1) * QW].astype(BF16)

        blocks(2 * ROWS, 64, w_out)

    def item_of(q, core, t):
        return (q * 2 + core) * NT + t

    def share(chip):
        rows = pl.ds(pl.multiple_of(chip * ITEM, ITEM), ITEM)
        own = jnp.dot(xc[rows], wc[...], preferred_element_type=F32) * scale
        for core in range(2):
            for q in range(NQ):
                at = core * HALF + q * QW
                part[item_of(q, core, chip)] = own[:, at : at + QW]

    for i in range(2, 5):
        local[i].wait()
        across[i].wait()
    share(z)
    for core in range(2):
        for q in range(NQ):
            at = core * HALF + q * QW
            n = item_of(q, core, z)
            part[n] = part[n] - tc[:, at : at + QW].astype(F32)

    def forward(j, cols):
        at = (pl.ds(pl.multiple_of(j * TOK, TOK), TOK), pl.ds(pl.multiple_of(cols * ROWS, ROWS), ROWS))
        return to_sibling(xc.at[at], xc.at[at], fwd_s.at[j], fwd_r.at[j])

    def pass_on(ahead):
        for i in range(2):
            dev, arrival = block(2 * ahead + i, False)
            arrival.wait_recv()
            forward(dev, c).start()

    def settle(ahead):
        for i in range(2):
            dev = far_device(i, CHIPS - ahead)
            forward(dev, c).wait_send()
            forward(dev, 1 - c).wait_recv()
            block(2 * ahead + i, True)[1].wait_send()
        share((z + CHIPS - ahead) % CHIPS)

    def arrive(ahead, carry):
        pass_on(ahead)
        pl.when(ahead > 1)(lambda: settle(ahead - 1))
        return carry

    lax.fori_loop(1, CHIPS, arrive, 0)
    settle(CHIPS - 1)
    if with_far:
        for q in range(NQ):
            send_far(NQ + q)

    def hop(n):
        return pltpu.make_async_remote_copy(
            src_ref=flow_out.at[n], dst_ref=flow_in.at[n], send_sem=flow_s.at[n], recv_sem=flow_r.at[n],
            device_id={"fsdp": (f + DEVS + 2 - 4 * c) % DEVS}, device_id_type=MESH,
        )

    def cross(m, n):
        return to_sibling(flow_in.at[n], cross_in.at[m], cross_s.at[m], cross_r.at[m])

    sems = ((g0_ss, g0_rs), (g1_ss, g1_rs))
    mixes = [
        Mix(g_raw.at[q], g_acc.at[q], g_send.at[q], g_recv.at[q], *sems[q], coef, 256) for q in range(NQ)
    ]

    def grad(q):
        turned = err[q * NT : (q + 1) * NT].reshape(DEVS * TOK, QW).T
        for k in range(4):
            size = 2 * ROWS // 4
            got = jnp.dot(turned, xc[:, k * size : (k + 1) * size], preferred_element_type=F32)
            g_raw[q, k * size : (k + 1) * size] = (got * scale).T.astype(BF16)
            mixes[q].begin(k)

    def advance(q, stage):
        for k in range(4):
            mixes[q].advance(k, stage)

    def moved_of(q, rows):
        cols = slice(q * QW, (q + 1) * QW)
        return 0.9 * wm_acc[pl.ds(2 * ROWS + rows.start, 64), cols] + g_acc[q, rows]

    out_cols = [pl.ds(pl.multiple_of(c * HALF + q * QW, QW), QW) for q in range(NQ)]
    o_rows = pl.ds(pl.multiple_of((1 - c) * ROWS, ROWS), ROWS)

    def ends(q):
        copies = []
        for i, out in enumerate((out_w, out_m)):
            at = out.at[0, :, out_cols[q]]
            k = 2 * q + i
            copies.append(to_sibling(fin.at[k, o_rows], at, fin_s.at[k], fin_r.at[k]))
            copies.append(pltpu.make_async_copy(fin.at[k, w_rows], at, fin_l.at[k]))
        return copies

    def mixed(q):
        if with_far:

            def body(rows):
                far_out[q, rows] = moved_of(q, rows).astype(BF16)

            blocks(2 * ROWS, 64, body)
            send_far(q)
        else:

            def body(rows):
                moved = moved_of(q, rows)
                fin[2 * q + 1, rows] = moved.astype(BF16)
                fin[2 * q, rows] = (wm_acc[rows, q * QW : (q + 1) * QW] - 0.05 * moved).astype(BF16)

            blocks(2 * ROWS, 64, body)
            for copy in ends(q):
                copy.start()

    def finish(q):
        if with_far:
            own, far = coef[FAR_LEVEL]
            if mode == FAR_HALF:
                for i in (NQ + q, q):
                    for p in range(pieces):
                        for k in range(len(SHARE_LEVELS)):
                            to_share(i, p, k).wait_recv()

            def shared_far(i, at):
                got = share_in[0, i, at]
                for k in range(1, len(SHARE_LEVELS)):
                    got = jnp.where(exponent[0] == SHARE_LEVELS[k], share_in[k, i, at], got)
                return got.astype(F32)

            def end(rows, far_of):
                moved = own * moved_of(q, rows) + far * far_of(q)
                kept = own * wm_acc[rows, q * QW : (q + 1) * QW] + far * far_of(NQ + q)
                fin[2 * q + 1, rows] = moved.astype(BF16)
                fin[2 * q, rows] = (kept - 0.05 * moved).astype(BF16)

            def direct(at):
                rows = pl.ds(pl.multiple_of(first_row + at.start, 64), 64)
                end(rows, lambda i: far_in[i, rows].astype(F32))

            def handed(at):
                rows = pl.ds(pl.multiple_of((1 - half) * ROWS + at.start, 64), 64)
                end(rows, lambda i: shared_far(i, at))

            blocks(pieces * PIECE, 64, direct)
            if mode == FAR_HALF:
                blocks(ROWS, 64, handed)
            for copy in ends(q):
                copy.start()

    def own_index(n):
        return n // (2 * NT) * NT + n % NT

    lag = SKEW * jnp.maximum(CHIPS - 1 - 2 * place, 0) + MARGIN
    late = jnp.logical_and(place > LATE, place < CHIPS - 1 - LATE)

    def step(s, carry):
        @pl.when(s < NITEM)
        def _():
            @pl.when(place > 0)
            def _():
                hop(s).wait_recv()

            @pl.when(place < CHIPS - 1)
            def _():
                flow_out[s] = (part[s] + flow_in[s].astype(F32)).astype(BF16)
                hop(s).start()

            @pl.when(jnp.logical_and(place > 0, s // NT % 2 != c))
            def _():
                cross(own_index(s), s).start()

        n = s - lag

        @pl.when(jnp.logical_and(jnp.logical_and(n >= 0, n < NITEM), n // NT % 2 == c))
        def _():
            m = own_index(n)

            @pl.when(place < CHIPS - 1)
            def _():
                cross(m, n).wait_recv()

            err[m] = (part[n] + flow_in[n].astype(F32) + cross_in[m].astype(F32)).astype(BF16)

        @pl.when(jnp.logical_not(late))
        def _():
            pl.when(n == 2 * NT)(lambda: grad(0))
            for stage in range(1, 5):
                pl.when(n == 2 * NT + GAP * stage)(lambda stage=stage: advance(0, stage))

        return carry

    steps = max(NITEM, 2 * NT + 4 * GAP + 1)
    lax.fori_loop(0, steps + SKEW * (CHIPS - 1) + MARGIN, step, 0)

    pl.when(late)(lambda: grad(0))
    grad(1)
    pl.when(jnp.logical_not(late))(lambda: mixed(0))
    for stage in range(1, 5):
        pl.when(late)(lambda stage=stage: advance(0, stage))
        advance(1, stage)
    pl.when(late)(lambda: mixed(0))
    mixed(1)

    def sent(n, carry):
        pl.when(place < CHIPS - 1)(lambda: hop(n).wait_send())
        pl.when(jnp.logical_and(place > 0, n // NT % 2 != c))(lambda: cross(own_index(n), n).wait_send())
        return carry

    lax.fori_loop(0, NITEM, sent, 0)
    for q in range(NQ):
        mixes[q].drain()
    if with_far:
        for q in range(NQ):
            hand_on(NQ + q)
    for q in range(NQ):
        if with_far:
            hand_on(q)
        finish(q)
    if with_far:
        for i in range(2 * NQ):
            for p in range(pieces):
                to_far(i, p).wait_send()
                if mode == FAR_HALF:
                    for k in range(len(SHARE_LEVELS)):
                        to_share(i, p, k).wait_send()
    for q in range(NQ):
        for copy in ends(q):
            copy.wait()


def step_call(mode, exponent, inputs, teacher, weight, momentum):
    dma = lambda *n: pltpu.SemaphoreType.DMA(n)
    anywhere = pl.BlockSpec(memory_space=pl.ANY)
    shape = jax.ShapeDtypeStruct((1, ROWS, KV), BF16)
    rows = 2 * ROWS
    far = 2 * NQ
    return pl.pallas_call(
        functools.partial(step_kernel, mode),
        name=("step_near", "step_far_whole", "step_far_half")[mode],
        out_shape=(shape, shape),
        in_specs=[pl.BlockSpec(memory_space=pltpu.SMEM)] + [anywhere] * 4,
        out_specs=(anywhere, anywhere),
        scratch_shapes=[
            pltpu.VMEM((DEVS * TOK, rows), BF16),
            pltpu.VMEM((2 * rows, HALF), BF16),
            pltpu.VMEM((rows, KV), BF16),
            pltpu.VMEM((2 * TOK, KV), BF16),
            pltpu.VMEM((2 * rows, HALF), F32),
            pltpu.VMEM((3, 2 * rows, HALF), BF16),
            pltpu.VMEM((4, 2 * rows, HALF), BF16),
            pltpu.VMEM((NITEM, ITEM, QW), F32),
            pltpu.VMEM((NITEM, ITEM, QW), BF16),
            pltpu.VMEM((NITEM, ITEM, QW), BF16),
            pltpu.VMEM((NOWN, ITEM, QW), BF16),
            pltpu.VMEM((NOWN, ITEM, QW), BF16),
            pltpu.VMEM((NQ, rows, QW), BF16),
            pltpu.VMEM((NQ, rows, QW), F32),
            pltpu.VMEM((NQ, 3, rows, QW), BF16),
            pltpu.VMEM((NQ, 4, rows, QW), BF16),
            pltpu.VMEM((2 * NQ, rows, QW), BF16),
            pltpu.VMEM((far, rows, QW), BF16),
            pltpu.VMEM((far, rows, QW), BF16),
            pltpu.VMEM((len(SHARE_LEVELS), far, ROWS, QW), BF16),
            dma(DEVS), dma(DEVS), dma(DEVS), dma(DEVS),
            dma(5), dma(5), dma(5),
            dma(4, 4), dma(4, 4), dma(4, 4), dma(4, 4), dma(4, 4), dma(4, 4),
            dma(NITEM), dma(NITEM), dma(NOWN), dma(NOWN),
            dma(2 * NQ), dma(2 * NQ), dma(2 * NQ),
            dma(far, rows // PIECE), dma(far, rows // PIECE),
            dma(len(SHARE_LEVELS), far, ROWS // PIECE), dma(len(SHARE_LEVELS), far, ROWS // PIECE),
        ],
        compiler_params=pltpu.CompilerParams(
            collective_id=mode, has_side_effects=True, vmem_limit_bytes=56 * 2**20
        ),
    )(exponent, inputs, teacher, weight, momentum)


def per_device(inputs, teacher, weight, momentum, exponent):
    far = jnp.where(exponent[0] == FAR_LEVEL, FAR_WHOLE, FAR_HALF)
    return lax.switch(
        jnp.where(jnp.any(exponent == FAR_LEVEL), far, NEAR),
        [lambda *args, mode=mode: tuple(step_call(mode, *args)) for mode in (NEAR, FAR_WHOLE, FAR_HALF)],
        exponent, inputs, teacher, weight, momentum,
    )


def solution(mesh):
    return jax.shard_map(
        per_device,
        mesh=mesh,
        in_specs=(
            P("group", "fsdp", None),
            P("group", "fsdp", None),
            P("group", "fsdp", None),
            P("group", "fsdp", None),
            P(),
        ),
        out_specs=(P("group", "fsdp", None), P("group", "fsdp", None)),
        check_vma=False,
    )
```
